32 devices in a mesh: rows: 8 (over z, x), dim: 4 (over y, core).
Axes of the slice: x: 2, y: 2, z: 4, core: 2. Of those that a mesh axis runs over, the one named last changes fastest.
Arguments:
- embeddings: float32 [64, 512, 128], P('rows', 'dim'), as said below
- prior: float32 [64, 512, 128], P('rows', 'dim'), may hold values from -9 to 9
- neighbours: int32 [64, 16], P('rows'), may hold values from 0 to 63, as said below
- seed_mask: int32 [8192], P('rows'), may hold values 0 or 1
- families: int32 [8192], P('rows'), may hold values from 0 to 511
Outputs:
- log_ratio: float32 [8192, 512], P(('rows', 'dim'))
The draws below stay inside these ranges and needn't reach their ends.
Inputs may be any that keep to these rules, and one draw needn't show every extreme that they name: `neighbours`: each list names 16 different blocks. Together, the lists of the 8 blocks 8g to 8g + 7 of one group name exactly 2 different blocks of every group of 8 blocks. `embeddings`: each row has its own positive scale.
All inputs are finite; a program needn't handle non-finite values. No bound on the sum of `seed_mask` on one device may be relied on, other than what follows from the above.
Results may differ from the reference program's by a relative error of at most 0.00078.
Values may be sent and summed in bfloat16 or wider, within the bound.
A program may use at most 64 MiB of HBM per device.

```python
import jax
import jax.numpy as jnp
from jax import lax

E = 512
F = 512
BR = 128
NBR = 16
ITERS = 3
GB = 8
NB = 64
N = 8192


def draw_embeddings(key, part):
    first, second, third = jax.random.split(key, 3)
    row_scale = jnp.exp(jax.random.uniform(first, (NB, 1, BR), jnp.float32, 0.0, 2.302585))
    col_scale = jnp.exp(jax.random.uniform(second, (1, E, 1), jnp.float32, 0.0, 2.302585))
    base = jax.random.normal(third, (NB, E, BR), jnp.float32)
    return (base * row_scale * col_scale).astype(jnp.float32)


def draw_neighbours(key, part):
    groups = NB // GB
    slots = GB // 4
    count = groups * slots
    cover = -(-count // NBR)

    def one_group(group_key):
        pick_key, order_key, heat_key, noise_key = jax.random.split(group_key, 4)
        chosen = jax.vmap(lambda inner: jax.random.permutation(inner, GB)[:slots])(jax.random.split(pick_key, groups))
        candidates = (jnp.arange(groups, dtype=jnp.int32)[:, None] * GB + chosen.astype(jnp.int32)).reshape(count)
        sigma = jax.random.permutation(order_key, count).astype(jnp.int32)
        places = jnp.arange(GB, dtype=jnp.int32)[:, None] * NBR + jnp.arange(NBR, dtype=jnp.int32)[None, :]
        cover_list = sigma[places % count]
        heat = jax.random.randint(heat_key, (count,), 0, 8)
        heat = heat * heat
        noise = jax.random.randint(noise_key, (GB, count), 0, 1024)
        score = (heat[None, :] * 1024 + noise) * count + jnp.arange(count, dtype=jnp.int32)[None, :]
        hot_list = lax.top_k(score, NBR)[1].astype(jnp.int32)
        picks = jnp.where(jnp.arange(GB, dtype=jnp.int32)[:, None] < cover, cover_list, hot_list)
        return candidates[picks]
    lists = jax.vmap(one_group)(jax.random.split(key, groups))
    return lists.reshape(NB, NBR).astype(jnp.int32)


def place_ends(values, own_key, least, largest):
    shape = values.shape
    place = [jax.random.randint(jax.random.fold_in(own_key, axis), (), 0, shape[axis]) for axis in range(len(shape))]
    values = values.at[tuple(place)].set(least)
    longest = shape.index(max(shape))
    place[longest] = (place[longest] + 1) % shape[longest]
    return values.at[tuple(place)].set(largest)


def block_levels(key, extent, pieces, least, high):
    loudness, own = 1.0, jax.random.fold_in(key, 6)
    for axis_at, shards_of in pieces:
        steps = jnp.exp(jax.random.uniform(jax.random.fold_in(own, axis_at), (shards_of,), jnp.float32, least / len(pieces), high / len(pieces)))
        loudness = loudness * jnp.repeat(steps, extent[axis_at] // shards_of).reshape([-1 if axis == axis_at else 1 for axis in range(len(extent))])
    return loudness


def normal_values(key, extent, scale, bound, cuts=(), kind=jnp.bfloat16):
    values = jax.random.normal(key, extent, jnp.float32) * scale
    if len(cuts) > 0:
        values = block_levels(key, extent, cuts, -0.22, 0.18) * values
    return jnp.clip(values, min=-bound, max=bound).astype(kind)


def setup_inputs(seed: int = 0) -> dict:
    key_of = jax.random.split(jax.random.key(seed), 6)
    embeddings = draw_embeddings(jax.random.fold_in(key_of[5], 71), 0)
    prior = normal_values(key_of[1], (NB, F, BR), 3.0, 9.0, ((0, 8), (1, 4)), jnp.float32)
    neighbours = draw_neighbours(jax.random.fold_in(key_of[5], 71), 0)
    seed_mask = place_ends((jax.random.randint(key_of[3], (N,), 0, 4) < 1).astype(jnp.int32), jax.random.fold_in(key_of[3], 1), 0, 1)
    families = place_ends(jax.random.randint(key_of[4], (N,), 0, F), jax.random.fold_in(key_of[4], 1), 0, F - 1).astype(jnp.int32)
    return {"embeddings": embeddings, "prior": prior, "neighbours": neighbours, "seed_mask": seed_mask, "families": families}


sharpness = 16.0
seed_weight = 0.5
label_floor = 0.001
norm_eps = 1e-06

def reference(embeddings, prior, neighbours, seed_mask, families):
    rows_major = jnp.transpose(embeddings, (0, 2, 1)).reshape(N, E)
    prior_rows = jnp.transpose(prior, (0, 2, 1)).reshape(N, F)
    squares = lax.optimization_barrier(jnp.sum(rows_major * rows_major, axis=1))
    unit = rows_major * lax.rsqrt(squares + norm_eps)[:, None]
    unit_blocks = unit.reshape(NB, BR, E)

    def block_weights(packed):
        query, listed = packed
        keys = unit_blocks[listed].reshape(NBR * BR, E)
        cosine = jnp.dot(query, keys.T, precision=lax.Precision.HIGHEST, preferred_element_type=jnp.float32)
        raised = jnp.exp(sharpness * (cosine - 1.0))
        return (raised / lax.optimization_barrier(jnp.sum(raised, axis=1, keepdims=True))).astype(jnp.bfloat16)
    weights = lax.map(block_weights, (unit_blocks, neighbours))
    raised_prior = jnp.exp(prior_rows)
    labels = (raised_prior / lax.optimization_barrier(jnp.sum(raised_prior, axis=1, keepdims=True))).astype(jnp.bfloat16)
    labels = labels.reshape(NB, BR, F)
    onehot = (families[:, None] == jnp.arange(F, dtype=jnp.int32)[None, :]).astype(jnp.float32)
    seeds = (seed_weight * seed_mask.astype(jnp.float32)[:, None] * onehot).reshape(NB, BR, F)
    shifted = seeds
    total = seeds
    for sweep in range(ITERS):
        current = labels

        def block_mix(packed):
            weight_block, listed = packed
            near_rows = current[listed].reshape(NBR * BR, F)
            return jnp.dot(weight_block, near_rows, preferred_element_type=jnp.float32)
        mixed = lax.map(block_mix, (weights, neighbours)) + seeds
        shifted = mixed + label_floor
        squared = shifted * shifted
        total = lax.optimization_barrier(jnp.sum(squared, axis=2, keepdims=True))
        if sweep + 1 < ITERS:
            labels = (squared / total).astype(jnp.bfloat16)
    result = 2.0 * jnp.log(shifted) - jnp.log(total) + jnp.log(jnp.float32(F))
    return result.reshape(N, F)
```

```python
import jax
import jax.numpy as jnp
from jax import lax
from jax.sharding import PartitionSpec as P

ITERS = 3


sharpness = 16.0
seed_weight = 0.5
label_floor = 0.001
norm_eps = 1e-06


def shards(embeddings, prior, neighbours, seed_mask, families):
    groups = lax.axis_size("rows")
    splits = lax.axis_size("dim")
    member = lax.axis_index("dim")
    blocks = neighbours.shape[0]
    links = neighbours.shape[1]
    width = embeddings.shape[1]
    block_rows = embeddings.shape[2]
    fam_part = prior.shape[1]
    fam_all = fam_part * splits
    slots = blocks // 4
    owned = blocks // splits
    candidates = groups * slots
    shared = candidates == links
    places = jnp.arange(blocks, dtype=jnp.int32)
    everything = groups * blocks
    hits = neighbours[:, :, None] == jnp.arange(everything, dtype=jnp.int32)[None, None, :]
    named = jnp.any(hits, axis=(0, 1)).reshape(groups, blocks)
    upto = (places[None, :] <= places[:, None]).astype(jnp.int32)
    order = jnp.sum(named.astype(jnp.int32)[:, None, :] * upto[None, :, :], axis=2) - 1
    chosen = named[:, None, :] & (order[:, None, :] == jnp.arange(slots, dtype=jnp.int32)[None, :, None])
    ranked = jnp.sum(jnp.where(chosen, places[None, None, :], 0), axis=2)
    wanted = lax.all_to_all(ranked, "rows", split_axis=0, concat_axis=0, tiled=True)
    local_squares = jnp.sum(embeddings * embeddings, axis=1)
    raised_prior = jnp.exp(prior)
    local_total = jnp.sum(raised_prior, axis=1)
    squares, prior_total = lax.psum((local_squares, local_total), "dim")
    unit_blocks = (embeddings * lax.rsqrt(squares + norm_eps)[:, None, :]).astype(jnp.bfloat16)
    labels = (raised_prior / prior_total[:, None, :]).astype(jnp.bfloat16)
    both = jnp.concatenate([unit_blocks, labels], axis=1)
    queries = lax.all_gather(unit_blocks, "dim", axis=1, tiled=True)
    arrived = lax.all_to_all(both[wanted], "rows", split_axis=0, concat_axis=0, tiled=True).reshape(
        candidates, width + fam_part, block_rows
    )
    came = arrived[:, width:]
    keys = lax.all_gather(arrived[:, :width], "dim", axis=1, tiled=True)
    if shared:
        cosine = jnp.einsum("sek,qer->skqr", keys, queries, preferred_element_type=jnp.float32)
        raised = jnp.exp(sharpness * (cosine - 1.0))
        weights = (raised / jnp.sum(raised, axis=(0, 1), keepdims=True)).astype(jnp.bfloat16)
    else:
        owner = neighbours // blocks
        within = neighbours % blocks
        match = (within[:, :, None] == places[None, None, :]).astype(jnp.int32)
        flat = owner * slots + jnp.sum(match * order[owner], axis=2)

        def block_weights(packed):
            query, listed = packed
            cosine = jnp.einsum(
                "sek,er->skr", keys[listed], query, preferred_element_type=jnp.float32
            )
            raised = jnp.exp(sharpness * (cosine - 1.0))
            return (raised / jnp.sum(raised, axis=(0, 1), keepdims=True)).astype(jnp.bfloat16)

        weights = lax.map(block_weights, (queries, flat))
    hot = families.reshape(blocks, 1, block_rows) - member * fam_part
    seeds = jnp.where(
        hot == jnp.arange(fam_part, dtype=jnp.int32)[None, :, None],
        seed_weight * seed_mask.astype(jnp.float32).reshape(blocks, 1, block_rows),
        0.0,
    )
    shifted = seeds
    for sweep in range(ITERS):
        if sweep > 0:
            came = lax.all_to_all(
                labels[wanted], "rows", split_axis=0, concat_axis=0, tiled=True
            ).reshape(candidates, fam_part, block_rows)
        if shared:
            mixed = jnp.einsum("sfk,skqr->qfr", came, weights, preferred_element_type=jnp.float32)
        else:
            near = came

            def block_mix(packed):
                weight, listed = packed
                return jnp.einsum(
                    "sfk,skr->fr", near[listed], weight, preferred_element_type=jnp.float32
                )

            mixed = lax.map(block_mix, (weights, flat))
        shifted = mixed + seeds + label_floor
        if sweep + 1 < ITERS:
            squared = shifted * shifted
            total = lax.psum(jnp.sum(squared, axis=1), "dim")
            labels = (squared / total[:, None, :]).astype(jnp.bfloat16)
    mine = lax.all_to_all(shifted, "dim", split_axis=0, concat_axis=1, tiled=True)
    total = jnp.sum(mine * mine, axis=1, keepdims=True)
    result = 2.0 * jnp.log(mine) - jnp.log(total) + jnp.log(jnp.float32(fam_all))
    return jnp.transpose(result, (0, 2, 1)).reshape(owned * block_rows, fam_all)


def solution(mesh):
    return jax.shard_map(
        shards,
        mesh=mesh,
        in_specs=(
            P("rows", "dim", None),
            P("rows", "dim", None),
            P("rows", None),
            P("rows"),
            P("rows"),
        ),
        out_specs=P(("rows", "dim"), None),
        check_vma=False,
    )
```

```python
import functools

import jax
import jax.numpy as jnp
from jax import lax
from jax.experimental import pallas as pl
from jax.experimental.pallas import tpu as pltpu
from jax.sharding import PartitionSpec as P

ITERS = 3


sharpness = 16.0
seed_weight = 0.5
label_floor = 0.001
norm_eps = 1e-06


def propagate(
    groups, splits, slots,
    wanted, unit, wide, labels, seeds, out,
    q_all, k_all, w_all, near, stage_u, stage_l, mixed, fresh, tot_mine, tot_got, fin_out,
    send_u, recv_u, send_l, recv_l, send_q, recv_q, send_k, recv_k, send_t, recv_t, send_f, recv_f,
):
    me = lax.axis_index("rows")
    member = lax.axis_index("dim")
    blocks, width, block_rows = unit.shape
    fam = labels.shape[1]
    rows = blocks * block_rows
    pair = slots * block_rows
    own = rows // splits
    bar = pltpu.get_barrier_semaphore()

    def row_peer(k):
        return {"rows": lax.rem(me + k, groups)}

    def dim_peer(j):
        return {"dim": lax.rem(member + j, splits)}

    def remote(src, dst, send, recv, peer):
        return pltpu.make_async_remote_copy(
            src_ref=src, dst_ref=dst, send_sem=send, recv_sem=recv,
            device_id=peer, device_id_type=pl.DeviceIdType.MESH,
        )

    def unit_copy(k):
        return remote(
            stage_u.at[k], k_all.at[k, pl.ds(0, width), :], send_u.at[k], recv_u.at[k], row_peer(k)
        )

    def label_copy(t, k):
        return remote(
            stage_l.at[t, k], near.at[t, k], send_l.at[t, k], recv_l.at[t, k], row_peer(k)
        )

    def query_copy(j):
        return remote(
            q_all.at[pl.ds(0, width), :], q_all.at[pl.ds(j * width, width), :],
            send_q.at[j], recv_q.at[j], dim_peer(j),
        )

    def key_copy(k, j):
        return remote(
            k_all.at[k, pl.ds(0, width), :], k_all.at[k, pl.ds(j * width, width), :],
            send_k.at[k, j], recv_k.at[k, j], dim_peer(j),
        )

    def total_copy(t, j):
        return remote(
            tot_mine.at[t], tot_got.at[t, j], send_t.at[t, j], recv_t.at[t, j], dim_peer(j)
        )

    def final_copy(j):
        return remote(
            fin_out.at[lax.rem(member + j, splits)], out.at[member], send_f.at[j], recv_f.at[j],
            dim_peer(j),
        )

    for k in range(1, groups):
        pl.semaphore_signal(bar, inc=1, device_id=row_peer(k), device_id_type=pl.DeviceIdType.MESH)
    for j in range(1, splits):
        pl.semaphore_signal(bar, inc=1, device_id=dim_peer(j), device_id_type=pl.DeviceIdType.MESH)

    q_all[0:width, :] = wide[...]

    def pick(k, s):
        return wanted[lax.rem(me + k, groups), s]

    for s in range(slots):
        k_all[0, 0:width, s * block_rows:(s + 1) * block_rows] = unit[pick(0, s)]
        near[0, 0, :, s * block_rows:(s + 1) * block_rows] = labels[pick(0, s)]
    pl.semaphore_wait(bar, groups + splits - 2)

    @pl.loop(1, groups)
    def _(k):
        for s in range(slots):
            stage_u[k, :, s * block_rows:(s + 1) * block_rows] = unit[pick(k, s)]
        unit_copy(k).start()

    for j in range(1, splits):
        query_copy(j).start()
    for j in range(1, splits):
        key_copy(0, j).start()

    @pl.loop(1, groups)
    def _(k):
        for s in range(slots):
            stage_l[0, k, :, s * block_rows:(s + 1) * block_rows] = labels[pick(k, s)]
        label_copy(0, k).start()

    for j in range(1, splits):
        query_copy(j).wait_recv()
    tot_mine[ITERS - 1] = jnp.zeros((1, rows), jnp.float32)

    def score(k):
        for j in range(1, splits):
            key_copy(k, j).wait_recv()

        @pl.loop(0, splits)
        def _(c):
            cols = pl.ds(pl.multiple_of(c * own, own), own)
            cosine = lax.dot_general(
                k_all[k], q_all[:, cols], (((0,), (0,)), ((), ())),
                preferred_element_type=jnp.float32,
            )
            raised = jnp.exp(sharpness * (cosine - 1.0))
            w_all[k, :, cols] = raised.astype(jnp.bfloat16)
            tot_mine[ITERS - 1, :, cols] += jnp.sum(raised, axis=0, keepdims=True)

    @pl.loop(1, groups)
    def _(k):
        unit_copy(k).wait_recv()
        for j in range(1, splits):
            key_copy(k, j).start()
        score(k - 1)

    score(groups - 1)

    for t in range(ITERS):
        mixed[...] = jnp.dot(near[t, 0], w_all[0], preferred_element_type=jnp.float32)

        @pl.loop(1, groups)
        def _(k):
            label_copy(t, k).wait_recv()
            mixed[...] += jnp.dot(near[t, k], w_all[k], preferred_element_type=jnp.float32)

        shifted = mixed[...] / tot_mine[ITERS - 1] + seeds[...] + label_floor
        if t + 1 < ITERS:
            squared = shifted * shifted
            mixed[...] = squared
            tot_mine[t] = jnp.sum(squared, axis=0, keepdims=True)
            for j in range(1, splits):
                total_copy(t, j).start()
            for j in range(1, splits):
                total_copy(t, j).wait_recv()
            total = tot_mine[t]
            for j in range(1, splits):
                total = total + tot_got[t, j]
            soft = (mixed[...] / total).astype(jnp.bfloat16)
            for b in range(blocks):
                fresh[t, b] = soft[:, b * block_rows:(b + 1) * block_rows]

            @pl.loop(1, groups)
            def _(k):
                for s in range(slots):
                    stage_l[t + 1, k, :, s * block_rows:(s + 1) * block_rows] = fresh[t, pick(k, s)]
                label_copy(t + 1, k).start()

            for s in range(slots):
                near[t + 1, 0, :, s * block_rows:(s + 1) * block_rows] = fresh[t, pick(0, s)]
        else:
            for m in range(splits):
                fin_out[m] = shifted[:, m * own:(m + 1) * own]
            for j in range(1, splits):
                final_copy(j).start()
            out[member] = fin_out[member]

    for j in range(1, splits):
        final_copy(j).wait_recv()
        final_copy(j).wait_send()
        query_copy(j).wait_send()
        key_copy(0, j).wait_send()
        for t in range(ITERS - 1):
            total_copy(t, j).wait_send()

    @pl.loop(1, groups)
    def _(k):
        unit_copy(k).wait_send()
        for j in range(1, splits):
            key_copy(k, j).wait_send()
        for t in range(ITERS):
            label_copy(t, k).wait_send()


def fused(groups, splits, slots, wanted, unit, wide, labels, seeds):
    blocks, width, block_rows = unit.shape
    fam = labels.shape[1]
    rows = blocks * block_rows
    pair = slots * block_rows
    own = rows // splits
    vmem = pl.BlockSpec(memory_space=pltpu.VMEM)
    dma = pltpu.SemaphoreType.DMA
    return pl.pallas_call(
        functools.partial(propagate, groups, splits, slots),
        out_shape=jax.ShapeDtypeStruct((splits, fam, own), jnp.float32),
        in_specs=[pl.BlockSpec(memory_space=pltpu.SMEM)] + [vmem] * 4,
        out_specs=vmem,
        scratch_shapes=[
            pltpu.VMEM((splits * width, rows), jnp.bfloat16),
            pltpu.VMEM((groups, splits * width, pair), jnp.bfloat16),
            pltpu.VMEM((groups, pair, rows), jnp.bfloat16),
            pltpu.VMEM((ITERS, groups, fam, pair), jnp.bfloat16),
            pltpu.VMEM((groups, width, pair), jnp.bfloat16),
            pltpu.VMEM((ITERS, groups, fam, pair), jnp.bfloat16),
            pltpu.VMEM((fam, rows), jnp.float32),
            pltpu.VMEM((ITERS - 1, blocks, fam, block_rows), jnp.bfloat16),
            pltpu.VMEM((ITERS, 1, rows), jnp.float32),
            pltpu.VMEM((ITERS - 1, splits, 1, rows), jnp.float32),
            pltpu.VMEM((splits, fam, own), jnp.float32),
            dma((groups,)), dma((groups,)),
            dma((ITERS, groups)), dma((ITERS, groups)),
            dma((splits,)), dma((splits,)),
            dma((groups, splits)), dma((groups, splits)),
            dma((ITERS - 1, splits)), dma((ITERS - 1, splits)),
            dma((splits,)), dma((splits,)),
        ],
        compiler_params=pltpu.CompilerParams(
            collective_id=0, has_side_effects=True, vmem_limit_bytes=40 * 1024 * 1024
        ),
    )(wanted, unit, wide, labels, seeds)


def finish(mine, fam_all):
    total = jnp.sum(mine * mine, axis=-2, keepdims=True)
    return 2.0 * jnp.log(mine) - jnp.log(total) + jnp.log(jnp.float32(fam_all))


def shards(embeddings, prior, neighbours, seed_mask, families):
    groups = lax.axis_size("rows")
    splits = lax.axis_size("dim")
    member = lax.axis_index("dim")
    blocks = neighbours.shape[0]
    links = neighbours.shape[1]
    width = embeddings.shape[1]
    block_rows = embeddings.shape[2]
    fam_part = prior.shape[1]
    fam_all = fam_part * splits
    slots = blocks // 4
    owned = blocks // splits
    candidates = groups * slots
    shared = candidates == links
    places = jnp.arange(blocks, dtype=jnp.int32)
    everything = groups * blocks
    hits = neighbours[:, :, None] == jnp.arange(everything, dtype=jnp.int32)[None, None, :]
    named = jnp.any(hits, axis=(0, 1)).reshape(groups, blocks)
    upto = (places[None, :] <= places[:, None]).astype(jnp.int32)
    order = jnp.sum(named.astype(jnp.int32)[:, None, :] * upto[None, :, :], axis=2) - 1
    chosen = named[:, None, :] & (order[:, None, :] == jnp.arange(slots, dtype=jnp.int32)[None, :, None])
    ranked = jnp.sum(jnp.where(chosen, places[None, None, :], 0), axis=2)
    wanted = lax.all_to_all(ranked, "rows", split_axis=0, concat_axis=0, tiled=True)
    local_squares = jnp.sum(embeddings * embeddings, axis=1)
    raised_prior = jnp.exp(prior)
    local_total = jnp.sum(raised_prior, axis=1)
    squares, prior_total = lax.psum((local_squares, local_total), "dim")
    unit_blocks = (embeddings * lax.rsqrt(squares + norm_eps)[:, None, :]).astype(jnp.bfloat16)
    labels = (raised_prior / prior_total[:, None, :]).astype(jnp.bfloat16)
    hot = families.reshape(blocks, 1, block_rows) - member * fam_part
    seeds = jnp.where(
        hot == jnp.arange(fam_part, dtype=jnp.int32)[None, :, None],
        seed_weight * seed_mask.astype(jnp.float32).reshape(blocks, 1, block_rows),
        0.0,
    )
    if shared:
        wide = jnp.transpose(unit_blocks, (1, 0, 2)).reshape(width, blocks * block_rows)
        seeds = jnp.transpose(seeds, (1, 0, 2)).reshape(fam_part, blocks * block_rows)
        mine = fused(groups, splits, slots, wanted, unit_blocks, wide, labels, seeds)
        return jnp.transpose(finish(mine.reshape(fam_all, owned * block_rows), fam_all))
    both = jnp.concatenate([unit_blocks, labels], axis=1)
    queries = lax.all_gather(unit_blocks, "dim", axis=1, tiled=True)
    arrived = lax.all_to_all(both[wanted], "rows", split_axis=0, concat_axis=0, tiled=True).reshape(
        candidates, width + fam_part, block_rows
    )
    came = arrived[:, width:]
    keys = lax.all_gather(arrived[:, :width], "dim", axis=1, tiled=True)
    owner = neighbours // blocks
    within = neighbours % blocks
    match = (within[:, :, None] == places[None, None, :]).astype(jnp.int32)
    flat = owner * slots + jnp.sum(match * order[owner], axis=2)

    def block_weights(packed):
        query, listed = packed
        cosine = jnp.einsum(
            "sek,er->skr", keys[listed], query, preferred_element_type=jnp.float32
        )
        raised = jnp.exp(sharpness * (cosine - 1.0))
        return (raised / jnp.sum(raised, axis=(0, 1), keepdims=True)).astype(jnp.bfloat16)

    weights = lax.map(block_weights, (queries, flat))
    shifted = seeds
    for sweep in range(ITERS):
        if sweep > 0:
            came = lax.all_to_all(
                labels[wanted], "rows", split_axis=0, concat_axis=0, tiled=True
            ).reshape(candidates, fam_part, block_rows)
        near = came

        def block_mix(packed):
            weight, listed = packed
            return jnp.einsum(
                "sfk,skr->fr", near[listed], weight, preferred_element_type=jnp.float32
            )

        mixed = lax.map(block_mix, (weights, flat))
        shifted = mixed + seeds + label_floor
        if sweep + 1 < ITERS:
            squared = shifted * shifted
            total = lax.psum(jnp.sum(squared, axis=1), "dim")
            labels = (squared / total[:, None, :]).astype(jnp.bfloat16)
    mine = lax.all_to_all(shifted, "dim", split_axis=0, concat_axis=1, tiled=True)
    result = finish(mine, fam_all)
    return jnp.transpose(result, (0, 2, 1)).reshape(owned * block_rows, fam_all)


def solution(mesh):
    return jax.shard_map(
        shards,
        mesh=mesh,
        in_specs=(
            P("rows", "dim", None),
            P("rows", "dim", None),
            P("rows", None),
            P("rows"),
            P("rows"),
        ),
        out_specs=P(("rows", "dim"), None),
        check_vma=False,
    )
```

```python
import functools

import jax
import jax.numpy as jnp
from jax import lax
from jax.experimental import pallas as pl
from jax.experimental.pallas import tpu as pltpu
from jax.sharding import PartitionSpec as P

ITERS = 3


sharpness = 16.0
seed_weight = 0.5
label_floor = 0.001
norm_eps = 1e-06


def propagate(
    groups, splits, slots,
    wanted, unit, wide, labels, seeds, out,
    q_all, k_all, raw, w_all, near, stage_u, stage_l, mixed, fresh, tot_mine, tot_got, fin_out,
    send_u, recv_u, send_l, recv_l, send_q, recv_q, send_k, recv_k, send_t, recv_t, send_f, recv_f,
):
    me = lax.axis_index("rows")
    member = lax.axis_index("dim")
    blocks, width, block_rows = unit.shape
    fam = labels.shape[1]
    rows = blocks * block_rows
    pair = slots * block_rows
    own = rows // splits
    bar = pltpu.get_barrier_semaphore()

    def row_peer(k):
        return {"rows": lax.rem(me + k, groups)}

    mate = member + 1 - 2 * lax.rem(member, 2)
    others = (member, mate, lax.rem(member + 2, splits), lax.rem(mate + 2, splits))

    def dim_peer(j):
        return {"dim": others[j]}

    def remote(src, dst, send, recv, peer):
        return pltpu.make_async_remote_copy(
            src_ref=src, dst_ref=dst, send_sem=send, recv_sem=recv,
            device_id=peer, device_id_type=pl.DeviceIdType.MESH,
        )

    def unit_copy(k):
        return remote(
            stage_u.at[k], k_all.at[k, pl.ds(0, width), :], send_u.at[k], recv_u.at[k], row_peer(k)
        )

    def label_copy(t, k):
        return remote(
            stage_l.at[t, k], near.at[t, k], send_l.at[t, k], recv_l.at[t, k], row_peer(k)
        )

    def query_copy(j):
        return remote(
            q_all.at[pl.ds((j // 3) * 2 * width, width), :], q_all.at[pl.ds(j * width, width), :],
            send_q.at[j], recv_q.at[j], dim_peer(2 if j == 2 else 1),
        )

    def key_copy(k, j):
        return remote(
            k_all.at[k, pl.ds((j // 3) * 2 * width, width), :],
            k_all.at[k, pl.ds(j * width, width), :],
            send_k.at[k, j], recv_k.at[k, j], dim_peer(2 if j == 2 else 1),
        )

    def total_copy(t, j):
        return remote(
            tot_mine.at[t], tot_got.at[t, j], send_t.at[t, j], recv_t.at[t, j], dim_peer(j)
        )

    def final_copy(j):
        return remote(
            fin_out.at[others[j]], out.at[member], send_f.at[j], recv_f.at[j],
            dim_peer(j),
        )

    for k in range(1, groups):
        pl.semaphore_signal(bar, inc=1, device_id=row_peer(k), device_id_type=pl.DeviceIdType.MESH)
    for j in range(1, splits):
        pl.semaphore_signal(bar, inc=1, device_id=dim_peer(j), device_id_type=pl.DeviceIdType.MESH)

    q_all[0:width, :] = wide[...]

    def pick(k, s):
        return wanted[lax.rem(me + k, groups), s]

    for s in range(slots):
        k_all[0, 0:width, s * block_rows:(s + 1) * block_rows] = unit[pick(0, s)]
        near[0, 0, :, s * block_rows:(s + 1) * block_rows] = labels[pick(0, s)]
    pl.semaphore_wait(bar, groups + splits - 2)

    @pl.loop(1, groups)
    def _(k):
        for s in range(slots):
            stage_u[k, :, s * block_rows:(s + 1) * block_rows] = unit[pick(k, s)]
        unit_copy(k).start()

    for j in (2, 1):
        query_copy(j).start()
    for j in (2, 1):
        key_copy(0, j).start()

    @pl.loop(1, groups)
    def _(k):
        for s in range(slots):
            stage_l[0, k, :, s * block_rows:(s + 1) * block_rows] = labels[pick(k, s)]
        label_copy(0, k).start()

    query_copy(2).wait_recv()
    query_copy(3).start()
    query_copy(1).wait_recv()
    query_copy(3).wait_recv()
    tot_mine[ITERS - 1] = jnp.zeros((1, rows), jnp.float32)

    def score(k):
        key_copy(k, 1).wait_recv()
        key_copy(k, 3).wait_recv()

        @pl.loop(0, splits)
        def _(c):
            cols = pl.ds(pl.multiple_of(c * own, own), own)
            cosine = lax.dot_general(
                k_all[k], q_all[:, cols], (((0,), (0,)), ((), ())),
                preferred_element_type=jnp.float32,
            )
            raised = jnp.exp(sharpness * (cosine - 1.0))
            raw[k, :, cols] = raised
            tot_mine[ITERS - 1, :, cols] += jnp.sum(raised, axis=0, keepdims=True)

    def spread(k):
        unit_copy(k).wait_recv()
        key_copy(k, 2).start()
        key_copy(k, 1).start()

    def hand_on(k):
        key_copy(k, 2).wait_recv()
        key_copy(k, 3).start()

    spread(1)
    hand_on(0)

    @pl.loop(2, groups)
    def _(k):
        spread(k)
        hand_on(k - 1)
        score(k - 2)

    hand_on(groups - 1)
    score(groups - 2)
    score(groups - 1)
    tot_mine[ITERS - 1] = 1.0 / tot_mine[ITERS - 1]

    @pl.loop(0, groups)
    def _(k):
        w_all[k] = (raw[k] * tot_mine[ITERS - 1]).astype(jnp.bfloat16)

    for t in range(ITERS):
        mixed[...] = jnp.dot(near[t, 0], w_all[0], preferred_element_type=jnp.float32)

        @pl.loop(1, groups)
        def _(k):
            label_copy(t, k).wait_recv()
            mixed[...] += jnp.dot(near[t, k], w_all[k], preferred_element_type=jnp.float32)

        shifted = mixed[...] + seeds[...] + label_floor
        if t + 1 < ITERS:
            squared = shifted * shifted
            mixed[...] = squared
            tot_mine[t] = jnp.sum(squared, axis=0, keepdims=True)
            for j in range(1, splits):
                total_copy(t, j).start()
            for j in range(1, splits):
                total_copy(t, j).wait_recv()
            total = tot_mine[t]
            for j in range(1, splits):
                total = total + tot_got[t, j]
            soft = (mixed[...] / total).astype(jnp.bfloat16)
            for b in range(blocks):
                fresh[t, b] = soft[:, b * block_rows:(b + 1) * block_rows]

            @pl.loop(1, groups)
            def _(k):
                for s in range(slots):
                    stage_l[t + 1, k, :, s * block_rows:(s + 1) * block_rows] = fresh[t, pick(k, s)]
                label_copy(t + 1, k).start()

            for s in range(slots):
                near[t + 1, 0, :, s * block_rows:(s + 1) * block_rows] = fresh[t, pick(0, s)]
        else:
            for m in range(splits):
                fin_out[m] = shifted[:, m * own:(m + 1) * own]
            for j in range(1, splits):
                final_copy(j).start()
            out[member] = fin_out[member]

    for j in range(1, splits):
        final_copy(j).wait_recv()
        final_copy(j).wait_send()
        query_copy(j).wait_send()
        key_copy(0, j).wait_send()
        for t in range(ITERS - 1):
            total_copy(t, j).wait_send()

    @pl.loop(1, groups)
    def _(k):
        unit_copy(k).wait_send()
        for j in range(1, splits):
            key_copy(k, j).wait_send()
        for t in range(ITERS):
            label_copy(t, k).wait_send()


def fused(groups, splits, slots, wanted, unit, wide, labels, seeds):
    blocks, width, block_rows = unit.shape
    fam = labels.shape[1]
    rows = blocks * block_rows
    pair = slots * block_rows
    own = rows // splits
    vmem = pl.BlockSpec(memory_space=pltpu.VMEM)
    dma = pltpu.SemaphoreType.DMA
    return pl.pallas_call(
        functools.partial(propagate, groups, splits, slots),
        out_shape=jax.ShapeDtypeStruct((splits, fam, own), jnp.float32),
        in_specs=[pl.BlockSpec(memory_space=pltpu.SMEM)] + [vmem] * 4,
        out_specs=vmem,
        scratch_shapes=[
            pltpu.VMEM((splits * width, rows), jnp.bfloat16),
            pltpu.VMEM((groups, splits * width, pair), jnp.bfloat16),
            pltpu.VMEM((groups, pair, rows), jnp.float32),
            pltpu.VMEM((groups, pair, rows), jnp.bfloat16),
            pltpu.VMEM((ITERS, groups, fam, pair), jnp.bfloat16),
            pltpu.VMEM((groups, width, pair), jnp.bfloat16),
            pltpu.VMEM((ITERS, groups, fam, pair), jnp.bfloat16),
            pltpu.VMEM((fam, rows), jnp.float32),
            pltpu.VMEM((ITERS - 1, blocks, fam, block_rows), jnp.bfloat16),
            pltpu.VMEM((ITERS, 1, rows), jnp.float32),
            pltpu.VMEM((ITERS - 1, splits, 1, rows), jnp.float32),
            pltpu.VMEM((splits, fam, own), jnp.float32),
            dma((groups,)), dma((groups,)),
            dma((ITERS, groups)), dma((ITERS, groups)),
            dma((splits,)), dma((splits,)),
            dma((groups, splits)), dma((groups, splits)),
            dma((ITERS - 1, splits)), dma((ITERS - 1, splits)),
            dma((splits,)), dma((splits,)),
        ],
        compiler_params=pltpu.CompilerParams(
            collective_id=0, has_side_effects=True, vmem_limit_bytes=40 * 1024 * 1024
        ),
    )(wanted, unit, wide, labels, seeds)


def finish(mine, fam_all):
    total = jnp.sum(mine * mine, axis=-2, keepdims=True)
    return 2.0 * jnp.log(mine) - jnp.log(total) + jnp.log(jnp.float32(fam_all))


def shards(embeddings, prior, neighbours, seed_mask, families):
    groups = lax.axis_size("rows")
    splits = lax.axis_size("dim")
    member = lax.axis_index("dim")
    blocks = neighbours.shape[0]
    links = neighbours.shape[1]
    width = embeddings.shape[1]
    block_rows = embeddings.shape[2]
    fam_part = prior.shape[1]
    fam_all = fam_part * splits
    slots = blocks // 4
    owned = blocks // splits
    candidates = groups * slots
    shared = candidates == links and splits == 4
    places = jnp.arange(blocks, dtype=jnp.int32)
    everything = groups * blocks
    hits = neighbours[:, :, None] == jnp.arange(everything, dtype=jnp.int32)[None, None, :]
    named = jnp.any(hits, axis=(0, 1)).reshape(groups, blocks)
    upto = (places[None, :] <= places[:, None]).astype(jnp.int32)
    order = jnp.sum(named.astype(jnp.int32)[:, None, :] * upto[None, :, :], axis=2) - 1
    chosen = named[:, None, :] & (order[:, None, :] == jnp.arange(slots, dtype=jnp.int32)[None, :, None])
    ranked = jnp.sum(jnp.where(chosen, places[None, None, :], 0), axis=2)
    wanted = lax.all_to_all(ranked, "rows", split_axis=0, concat_axis=0, tiled=True)
    local_squares = jnp.sum(embeddings * embeddings, axis=1)
    raised_prior = jnp.exp(prior)
    local_total = jnp.sum(raised_prior, axis=1)
    squares, prior_total = lax.psum((local_squares, local_total), "dim")
    unit_blocks = (embeddings * lax.rsqrt(squares + norm_eps)[:, None, :]).astype(jnp.bfloat16)
    labels = (raised_prior / prior_total[:, None, :]).astype(jnp.bfloat16)
    hot = families.reshape(blocks, 1, block_rows) - member * fam_part
    seeds = jnp.where(
        hot == jnp.arange(fam_part, dtype=jnp.int32)[None, :, None],
        seed_weight * seed_mask.astype(jnp.float32).reshape(blocks, 1, block_rows),
        0.0,
    )
    if shared:
        wide = jnp.transpose(unit_blocks, (1, 0, 2)).reshape(width, blocks * block_rows)
        seeds = jnp.transpose(seeds, (1, 0, 2)).reshape(fam_part, blocks * block_rows)
        mine = fused(groups, splits, slots, wanted, unit_blocks, wide, labels, seeds)
        return jnp.transpose(finish(mine.reshape(fam_all, owned * block_rows), fam_all))
    both = jnp.concatenate([unit_blocks, labels], axis=1)
    queries = lax.all_gather(unit_blocks, "dim", axis=1, tiled=True)
    arrived = lax.all_to_all(both[wanted], "rows", split_axis=0, concat_axis=0, tiled=True).reshape(
        candidates, width + fam_part, block_rows
    )
    came = arrived[:, width:]
    keys = lax.all_gather(arrived[:, :width], "dim", axis=1, tiled=True)
    owner = neighbours // blocks
    within = neighbours % blocks
    match = (within[:, :, None] == places[None, None, :]).astype(jnp.int32)
    flat = owner * slots + jnp.sum(match * order[owner], axis=2)

    def block_weights(packed):
        query, listed = packed
        cosine = jnp.einsum(
            "sek,er->skr", keys[listed], query, preferred_element_type=jnp.float32
        )
        raised = jnp.exp(sharpness * (cosine - 1.0))
        return (raised / jnp.sum(raised, axis=(0, 1), keepdims=True)).astype(jnp.bfloat16)

    weights = lax.map(block_weights, (queries, flat))
    shifted = seeds
    for sweep in range(ITERS):
        if sweep > 0:
            came = lax.all_to_all(
                labels[wanted], "rows", split_axis=0, concat_axis=0, tiled=True
            ).reshape(candidates, fam_part, block_rows)
        near = came

        def block_mix(packed):
            weight, listed = packed
            return jnp.einsum(
                "sfk,skr->fr", near[listed], weight, preferred_element_type=jnp.float32
            )

        mixed = lax.map(block_mix, (weights, flat))
        shifted = mixed + seeds + label_floor
        if sweep + 1 < ITERS:
            squared = shifted * shifted
            total = lax.psum(jnp.sum(squared, axis=1), "dim")
            labels = (squared / total[:, None, :]).astype(jnp.bfloat16)
    mine = lax.all_to_all(shifted, "dim", split_axis=0, concat_axis=1, tiled=True)
    result = finish(mine, fam_all)
    return jnp.transpose(result, (0, 2, 1)).reshape(owned * block_rows, fam_all)


def solution(mesh):
    return jax.shard_map(
        shards,
        mesh=mesh,
        in_specs=(
            P("rows", "dim", None),
            P("rows", "dim", None),
            P("rows", None),
            P("rows"),
            P("rows"),
        ),
        out_specs=P(("rows", "dim"), None),
        check_vma=False,
    )
```

```python
import functools

import jax
import jax.numpy as jnp
from jax import lax
from jax.experimental import pallas as pl
from jax.experimental.pallas import tpu as pltpu
from jax.sharding import PartitionSpec as P

ITERS = 3


sharpness = 16.0
seed_weight = 0.5
label_floor = 0.001
norm_eps = 1e-06


def propagate(
    groups, splits, slots,
    ranks, emb, prior, seeds, out,
    unit, labels, pre_mine, pre_got, rank_got, wanted,
    q_all, k_all, raw, w_all, near, stage_u, stage_l, mixed, fresh, tot_mine, tot_got, fin_out,
    send_u, recv_u, send_l, recv_l, send_q, recv_q, send_k, recv_k, send_t, recv_t, send_f, recv_f,
    send_p, recv_p, send_r, recv_r, move,
):
    me = lax.axis_index("rows")
    member = lax.axis_index("dim")
    blocks, width, block_rows = emb.shape
    rows = blocks * block_rows
    own = rows // splits
    bar = pltpu.get_barrier_semaphore()

    def row_peer(k):
        return {"rows": lax.rem(me + k, groups)}

    mate = member + 1 - 2 * lax.rem(member, 2)
    others = (member, mate, lax.rem(member + 2, splits), lax.rem(mate + 2, splits))

    def dim_peer(j):
        return {"dim": others[j]}

    def remote(src, dst, send, recv, peer):
        return pltpu.make_async_remote_copy(
            src_ref=src, dst_ref=dst, send_sem=send, recv_sem=recv,
            device_id=peer, device_id_type=pl.DeviceIdType.MESH,
        )

    def unit_copy(k):
        return remote(
            stage_u.at[k], k_all.at[k, pl.ds(0, width), :], send_u.at[k], recv_u.at[k], row_peer(k)
        )

    def label_copy(t, k):
        return remote(
            stage_l.at[t, k], near.at[t, k], send_l.at[t, k], recv_l.at[t, k], row_peer(k)
        )

    def query_copy(j):
        return remote(
            q_all.at[pl.ds((j // 3) * 2 * width, width), :], q_all.at[pl.ds(j * width, width), :],
            send_q.at[j], recv_q.at[j], dim_peer(2 if j == 2 else 1),
        )

    def key_copy(k, j):
        return remote(
            k_all.at[k, pl.ds((j // 3) * 2 * width, width), :],
            k_all.at[k, pl.ds(j * width, width), :],
            send_k.at[k, j], recv_k.at[k, j], dim_peer(2 if j == 2 else 1),
        )

    def total_copy(t, j):
        return remote(
            tot_mine.at[t], tot_got.at[t, j], send_t.at[t, j], recv_t.at[t, j], dim_peer(j)
        )

    def pre_copy(j):
        return remote(pre_mine, pre_got.at[j], send_p.at[j], recv_p.at[j], dim_peer(j))

    def rank_copy(k):
        return remote(
            ranks.at[lax.rem(me + k, groups)], rank_got.at[me], send_r.at[k], recv_r.at[k],
            row_peer(k),
        )

    def final_copy(j):
        return remote(
            fin_out.at[others[j]], out.at[member], send_f.at[j], recv_f.at[j],
            dim_peer(j),
        )

    for k in range(1, groups):
        pl.semaphore_signal(bar, inc=1, device_id=row_peer(k), device_id_type=pl.DeviceIdType.MESH)
    for j in range(1, splits):
        pl.semaphore_signal(bar, inc=1, device_id=dim_peer(j), device_id_type=pl.DeviceIdType.MESH)

    rank_got[me] = ranks[me]
    for b in range(blocks):
        values = emb[b]
        pre_mine[0, b:b + 1, :] = jnp.sum(values * values, axis=0, keepdims=True)
        pre_mine[1, b:b + 1, :] = jnp.sum(jnp.exp(prior[b]), axis=0, keepdims=True)
    pl.semaphore_wait(bar, groups + splits - 2)
    for k in range(1, groups):
        rank_copy(k).start()
    for j in range(1, splits):
        pre_copy(j).start()
    for j in range(1, splits):
        pre_copy(j).wait_recv()
    sums = pre_mine[...]
    for j in range(1, splits):
        sums = sums + pre_got[j]
    scale = lax.rsqrt(sums[0] + norm_eps)
    for b in range(blocks):
        slices = (emb[b] * scale[b:b + 1, :]).astype(jnp.bfloat16)
        unit[b] = slices
        q_all[0:width, b * block_rows:(b + 1) * block_rows] = slices
    for j in (2, 1):
        query_copy(j).start()
    for k in range(1, groups):
        rank_copy(k).wait_recv()
    down = pltpu.make_async_copy(rank_got, wanted, move.at[0])
    down.start()
    down.wait()

    def pick(k, s):
        return wanted[lax.rem(me + k, groups), 0, s]

    @pl.loop(1, groups)
    def _(k):
        for s in range(slots):
            stage_u[k, :, s * block_rows:(s + 1) * block_rows] = unit[pick(k, s)]
        unit_copy(k).start()

    for s in range(slots):
        k_all[0, 0:width, s * block_rows:(s + 1) * block_rows] = unit[pick(0, s)]
    for j in (2, 1):
        key_copy(0, j).start()
    for b in range(blocks):
        labels[b] = (jnp.exp(prior[b]) / sums[1, b:b + 1, :]).astype(jnp.bfloat16)
    for s in range(slots):
        near[0, 0, :, s * block_rows:(s + 1) * block_rows] = labels[pick(0, s)]

    @pl.loop(1, groups)
    def _(k):
        for s in range(slots):
            stage_l[0, k, :, s * block_rows:(s + 1) * block_rows] = labels[pick(k, s)]
        label_copy(0, k).start()

    query_copy(2).wait_recv()
    query_copy(3).start()
    query_copy(1).wait_recv()
    query_copy(3).wait_recv()
    tot_mine[ITERS - 1] = jnp.zeros((1, rows), jnp.float32)

    def score(k):
        key_copy(k, 1).wait_recv()
        key_copy(k, 3).wait_recv()

        @pl.loop(0, splits)
        def _(c):
            cols = pl.ds(pl.multiple_of(c * own, own), own)
            cosine = lax.dot_general(
                k_all[k], q_all[:, cols], (((0,), (0,)), ((), ())),
                preferred_element_type=jnp.float32,
            )
            raised = jnp.exp(sharpness * (cosine - 1.0))
            raw[k, :, cols] = raised
            tot_mine[ITERS - 1, :, cols] += jnp.sum(raised, axis=0, keepdims=True)

    def spread(k):
        unit_copy(k).wait_recv()
        key_copy(k, 2).start()
        key_copy(k, 1).start()

    def hand_on(k):
        key_copy(k, 2).wait_recv()
        key_copy(k, 3).start()

    spread(1)
    hand_on(0)

    @pl.loop(2, groups)
    def _(k):
        spread(k)
        hand_on(k - 1)
        score(k - 2)

    hand_on(groups - 1)
    score(groups - 2)
    score(groups - 1)
    tot_mine[ITERS - 1] = 1.0 / tot_mine[ITERS - 1]

    @pl.loop(0, groups)
    def _(k):
        w_all[k] = (raw[k] * tot_mine[ITERS - 1]).astype(jnp.bfloat16)

    for t in range(ITERS):
        mixed[...] = jnp.dot(near[t, 0], w_all[0], preferred_element_type=jnp.float32)

        @pl.loop(1, groups)
        def _(k):
            label_copy(t, k).wait_recv()
            mixed[...] += jnp.dot(near[t, k], w_all[k], preferred_element_type=jnp.float32)

        shifted = mixed[...] + seeds[...] + label_floor
        if t + 1 < ITERS:
            squared = shifted * shifted
            mixed[...] = squared
            tot_mine[t] = jnp.sum(squared, axis=0, keepdims=True)
            for j in range(1, splits):
                total_copy(t, j).start()
            for j in range(1, splits):
                total_copy(t, j).wait_recv()
            total = tot_mine[t]
            for j in range(1, splits):
                total = total + tot_got[t, j]
            soft = (mixed[...] / total).astype(jnp.bfloat16)
            for b in range(blocks):
                fresh[t, b] = soft[:, b * block_rows:(b + 1) * block_rows]

            @pl.loop(1, groups)
            def _(k):
                for s in range(slots):
                    stage_l[t + 1, k, :, s * block_rows:(s + 1) * block_rows] = fresh[t, pick(k, s)]
                label_copy(t + 1, k).start()

            for s in range(slots):
                near[t + 1, 0, :, s * block_rows:(s + 1) * block_rows] = fresh[t, pick(0, s)]
        else:
            for m in range(splits):
                fin_out[m] = shifted[:, m * own:(m + 1) * own]
            for j in range(1, splits):
                final_copy(j).start()
            out[member] = fin_out[member]

    for j in range(1, splits):
        final_copy(j).wait_recv()
        final_copy(j).wait_send()
        query_copy(j).wait_send()
        pre_copy(j).wait_send()
        key_copy(0, j).wait_send()
        for t in range(ITERS - 1):
            total_copy(t, j).wait_send()

    @pl.loop(1, groups)
    def _(k):
        rank_copy(k).wait_send()
        unit_copy(k).wait_send()
        for j in range(1, splits):
            key_copy(k, j).wait_send()
        for t in range(ITERS):
            label_copy(t, k).wait_send()


def fused(groups, splits, slots, ranks, emb, prior, seeds):
    blocks, width, block_rows = emb.shape
    fam = prior.shape[1]
    rows = blocks * block_rows
    pair = slots * block_rows
    own = rows // splits
    vmem = pl.BlockSpec(memory_space=pltpu.VMEM)
    dma = pltpu.SemaphoreType.DMA
    return pl.pallas_call(
        functools.partial(propagate, groups, splits, slots),
        out_shape=jax.ShapeDtypeStruct((splits, fam, own), jnp.float32),
        in_specs=[vmem] * 4,
        out_specs=vmem,
        scratch_shapes=[
            pltpu.VMEM((blocks, width, block_rows), jnp.bfloat16),
            pltpu.VMEM((blocks, fam, block_rows), jnp.bfloat16),
            pltpu.VMEM((2, blocks, block_rows), jnp.float32),
            pltpu.VMEM((splits, 2, blocks, block_rows), jnp.float32),
            pltpu.VMEM((groups, 1, 128), jnp.int32),
            pltpu.SMEM((groups, 1, 128), jnp.int32),
            pltpu.VMEM((splits * width, rows), jnp.bfloat16),
            pltpu.VMEM((groups, splits * width, pair), jnp.bfloat16),
            pltpu.VMEM((groups, pair, rows), jnp.float32),
            pltpu.VMEM((groups, pair, rows), jnp.bfloat16),
            pltpu.VMEM((ITERS, groups, fam, pair), jnp.bfloat16),
            pltpu.VMEM((groups, width, pair), jnp.bfloat16),
            pltpu.VMEM((ITERS, groups, fam, pair), jnp.bfloat16),
            pltpu.VMEM((fam, rows), jnp.float32),
            pltpu.VMEM((ITERS - 1, blocks, fam, block_rows), jnp.bfloat16),
            pltpu.VMEM((ITERS, 1, rows), jnp.float32),
            pltpu.VMEM((ITERS - 1, splits, 1, rows), jnp.float32),
            pltpu.VMEM((splits, fam, own), jnp.float32),
            dma((groups,)), dma((groups,)),
            dma((ITERS, groups)), dma((ITERS, groups)),
            dma((splits,)), dma((splits,)),
            dma((groups, splits)), dma((groups, splits)),
            dma((ITERS - 1, splits)), dma((ITERS - 1, splits)),
            dma((splits,)), dma((splits,)),
            dma((splits,)), dma((splits,)), dma((groups,)), dma((groups,)), dma((1,)),
        ],
        compiler_params=pltpu.CompilerParams(
            collective_id=0, has_side_effects=True, vmem_limit_bytes=40 * 1024 * 1024
        ),
    )(ranks, emb, prior, seeds)


def finish(mine, fam_all):
    total = jnp.sum(mine * mine, axis=-2, keepdims=True)
    return 2.0 * jnp.log(mine) - jnp.log(total) + jnp.log(jnp.float32(fam_all))


def shards(embeddings, prior, neighbours, seed_mask, families):
    groups = lax.axis_size("rows")
    splits = lax.axis_size("dim")
    member = lax.axis_index("dim")
    blocks = neighbours.shape[0]
    links = neighbours.shape[1]
    width = embeddings.shape[1]
    block_rows = embeddings.shape[2]
    fam_part = prior.shape[1]
    fam_all = fam_part * splits
    slots = blocks // 4
    owned = blocks // splits
    candidates = groups * slots
    shared = candidates == links and splits == 4
    places = jnp.arange(blocks, dtype=jnp.int32)
    everything = groups * blocks
    hits = neighbours[:, :, None] == jnp.arange(everything, dtype=jnp.int32)[None, None, :]
    named = jnp.any(hits, axis=(0, 1)).reshape(groups, blocks)
    upto = (places[None, :] <= places[:, None]).astype(jnp.int32)
    order = jnp.sum(named.astype(jnp.int32)[:, None, :] * upto[None, :, :], axis=2) - 1
    chosen = named[:, None, :] & (order[:, None, :] == jnp.arange(slots, dtype=jnp.int32)[None, :, None])
    ranked = jnp.sum(jnp.where(chosen, places[None, None, :], 0), axis=2)
    hot = families.reshape(blocks, 1, block_rows) - member * fam_part
    seeds = jnp.where(
        hot == jnp.arange(fam_part, dtype=jnp.int32)[None, :, None],
        seed_weight * seed_mask.astype(jnp.float32).reshape(blocks, 1, block_rows),
        0.0,
    )
    if shared:
        seeds = jnp.transpose(seeds, (1, 0, 2)).reshape(fam_part, blocks * block_rows)
        ranks = jnp.pad(ranked, ((0, 0), (0, 128 - slots)))[:, None, :]
        mine = fused(groups, splits, slots, ranks, embeddings, prior, seeds)
        return jnp.transpose(finish(mine.reshape(fam_all, owned * block_rows), fam_all))
    wanted = lax.all_to_all(ranked, "rows", split_axis=0, concat_axis=0, tiled=True)
    local_squares = jnp.sum(embeddings * embeddings, axis=1)
    raised_prior = jnp.exp(prior)
    local_total = jnp.sum(raised_prior, axis=1)
    squares, prior_total = lax.psum((local_squares, local_total), "dim")
    unit_blocks = (embeddings * lax.rsqrt(squares + norm_eps)[:, None, :]).astype(jnp.bfloat16)
    labels = (raised_prior / prior_total[:, None, :]).astype(jnp.bfloat16)
    both = jnp.concatenate([unit_blocks, labels], axis=1)
    queries = lax.all_gather(unit_blocks, "dim", axis=1, tiled=True)
    arrived = lax.all_to_all(both[wanted], "rows", split_axis=0, concat_axis=0, tiled=True).reshape(
        candidates, width + fam_part, block_rows
    )
    came = arrived[:, width:]
    keys = lax.all_gather(arrived[:, :width], "dim", axis=1, tiled=True)
    owner = neighbours // blocks
    within = neighbours % blocks
    match = (within[:, :, None] == places[None, None, :]).astype(jnp.int32)
    flat = owner * slots + jnp.sum(match * order[owner], axis=2)

    def block_weights(packed):
        query, listed = packed
        cosine = jnp.einsum(
            "sek,er->skr", keys[listed], query, preferred_element_type=jnp.float32
        )
        raised = jnp.exp(sharpness * (cosine - 1.0))
        return (raised / jnp.sum(raised, axis=(0, 1), keepdims=True)).astype(jnp.bfloat16)

    weights = lax.map(block_weights, (queries, flat))
    shifted = seeds
    for sweep in range(ITERS):
        if sweep > 0:
            came = lax.all_to_all(
                labels[wanted], "rows", split_axis=0, concat_axis=0, tiled=True
            ).reshape(candidates, fam_part, block_rows)
        near = came

        def block_mix(packed):
            weight, listed = packed
            return jnp.einsum(
                "sfk,skr->fr", near[listed], weight, preferred_element_type=jnp.float32
            )

        mixed = lax.map(block_mix, (weights, flat))
        shifted = mixed + seeds + label_floor
        if sweep + 1 < ITERS:
            squared = shifted * shifted
            total = lax.psum(jnp.sum(squared, axis=1), "dim")
            labels = (squared / total[:, None, :]).astype(jnp.bfloat16)
    mine = lax.all_to_all(shifted, "dim", split_axis=0, concat_axis=1, tiled=True)
    result = finish(mine, fam_all)
    return jnp.transpose(result, (0, 2, 1)).reshape(owned * block_rows, fam_all)


def solution(mesh):
    return jax.shard_map(
        shards,
        mesh=mesh,
        in_specs=(
            P("rows", "dim", None),
            P("rows", "dim", None),
            P("rows", None),
            P("rows"),
            P("rows"),
        ),
        out_specs=P(("rows", "dim"), None),
        check_vma=False,
    )
```

```python
import functools

import jax
import jax.numpy as jnp
from jax import lax
from jax.experimental import pallas as pl
from jax.experimental.pallas import tpu as pltpu
from jax.sharding import PartitionSpec as P

ITERS = 3


sharpness = 16.0
seed_weight = 0.5
label_floor = 0.001
norm_eps = 1e-06


def propagate(
    groups, splits, slots,
    ranks, emb, prior, seeds, out,
    unit, labels, pre_mine, pre_got, rank_got, wanted,
    q_all, k_all, turned, raw, w_all, near, stage_u, stage_l, mixed, fresh, tot_mine, tot_got, fin_out,
    send_u, recv_u, send_l, recv_l, send_q, recv_q, send_k, recv_k, send_t, recv_t, send_f, recv_f,
    send_p, recv_p, send_r, recv_r, move,
):
    me = lax.axis_index("rows")
    member = lax.axis_index("dim")
    blocks, width, block_rows = emb.shape
    rows = blocks * block_rows
    own = rows // splits
    bar = pltpu.get_barrier_semaphore()

    def row_peer(k):
        return {"rows": lax.rem(me + k, groups)}

    mate = member + 1 - 2 * lax.rem(member, 2)
    others = (member, mate, lax.rem(member + 2, splits), lax.rem(mate + 2, splits))

    def dim_peer(j):
        return {"dim": others[j]}

    def remote(src, dst, send, recv, peer):
        return pltpu.make_async_remote_copy(
            src_ref=src, dst_ref=dst, send_sem=send, recv_sem=recv,
            device_id=peer, device_id_type=pl.DeviceIdType.MESH,
        )

    def unit_copy(k):
        return remote(
            stage_u.at[k], k_all.at[k, pl.ds(0, width), :], send_u.at[k], recv_u.at[k], row_peer(k)
        )

    def label_copy(t, k):
        return remote(
            stage_l.at[t, k], near.at[t, k], send_l.at[t, k], recv_l.at[t, k], row_peer(k)
        )

    def query_copy(j):
        return remote(
            q_all.at[pl.ds((j // 3) * 2 * width, width), :], q_all.at[pl.ds(j * width, width), :],
            send_q.at[j], recv_q.at[j], dim_peer(2 if j == 2 else 1),
        )

    def key_copy(k, j):
        return remote(
            k_all.at[k, pl.ds((j // 3) * 2 * width, width), :],
            k_all.at[k, pl.ds(j * width, width), :],
            send_k.at[k, j], recv_k.at[k, j], dim_peer(2 if j == 2 else 1),
        )

    def total_copy(t, j):
        return remote(
            tot_mine.at[t], tot_got.at[t, j], send_t.at[t, j], recv_t.at[t, j], dim_peer(j)
        )

    def pre_copy(j):
        return remote(pre_mine, pre_got.at[j], send_p.at[j], recv_p.at[j], dim_peer(j))

    def rank_copy(k):
        return remote(
            ranks.at[lax.rem(me + k, groups)], rank_got.at[me], send_r.at[k], recv_r.at[k],
            row_peer(k),
        )

    def final_copy(j):
        return remote(
            fin_out.at[others[j]], out.at[member], send_f.at[j], recv_f.at[j],
            dim_peer(j),
        )

    for k in range(1, groups):
        pl.semaphore_signal(bar, inc=1, device_id=row_peer(k), device_id_type=pl.DeviceIdType.MESH)
    for j in range(1, splits):
        pl.semaphore_signal(bar, inc=1, device_id=dim_peer(j), device_id_type=pl.DeviceIdType.MESH)

    rank_got[me] = ranks[me]
    for b in range(blocks):
        values = emb[b]
        pre_mine[0, b:b + 1, :] = jnp.sum(values * values, axis=0, keepdims=True)
        pre_mine[1, b:b + 1, :] = jnp.sum(jnp.exp(prior[b]), axis=0, keepdims=True)
    pl.semaphore_wait(bar, groups + splits - 2)
    for k in range(1, groups):
        rank_copy(k).start()
    for j in range(1, splits):
        pre_copy(j).start()
    for j in range(1, splits):
        pre_copy(j).wait_recv()
    sums = pre_mine[...]
    for j in range(1, splits):
        sums = sums + pre_got[j]
    scale = lax.rsqrt(sums[0] + norm_eps)
    for b in range(blocks):
        slices = (emb[b] * scale[b:b + 1, :]).astype(jnp.bfloat16)
        unit[b] = slices
        q_all[0:width, b * block_rows:(b + 1) * block_rows] = slices
    for j in (2, 1):
        query_copy(j).start()
    for k in range(1, groups):
        rank_copy(k).wait_recv()
    down = pltpu.make_async_copy(rank_got, wanted, move.at[0])
    down.start()
    down.wait()

    def pick(k, s):
        return wanted[lax.rem(me + k, groups), 0, s]

    @pl.loop(1, groups)
    def _(k):
        for s in range(slots):
            stage_u[k, :, s * block_rows:(s + 1) * block_rows] = unit[pick(k, s)]
        unit_copy(k).start()

    for s in range(slots):
        k_all[0, 0:width, s * block_rows:(s + 1) * block_rows] = unit[pick(0, s)]
    for j in (2, 1):
        key_copy(0, j).start()
    for b in range(blocks):
        labels[b] = (jnp.exp(prior[b]) / sums[1, b:b + 1, :]).astype(jnp.bfloat16)
    for s in range(slots):
        near[0, 0, :, s * block_rows:(s + 1) * block_rows] = labels[pick(0, s)]

    @pl.loop(1, groups)
    def _(k):
        for s in range(slots):
            stage_l[0, k, :, s * block_rows:(s + 1) * block_rows] = labels[pick(k, s)]

    query_copy(2).wait_recv()
    query_copy(3).start()
    query_copy(1).wait_recv()
    query_copy(3).wait_recv()
    tot_mine[ITERS - 1] = jnp.zeros((1, rows), jnp.float32)

    def score(k):
        key_copy(k, 1).wait_recv()
        key_copy(k, 3).wait_recv()
        turned[...] = k_all[k].T

        @pl.loop(0, splits)
        def _(c):
            cols = pl.ds(pl.multiple_of(c * own, own), own)
            cosine = lax.dot_general(
                turned[...], q_all[:, cols], (((1,), (0,)), ((), ())),
                preferred_element_type=jnp.float32,
            )
            raised = jnp.exp(sharpness * (cosine - 1.0))
            raw[k, :, cols] = raised
            tot_mine[ITERS - 1, :, cols] += jnp.sum(raised, axis=0, keepdims=True)

    def spread(k):
        unit_copy(k).wait_recv()
        key_copy(k, 2).start()
        key_copy(k, 1).start()
        label_copy(0, k).start()

    def hand_on(k):
        key_copy(k, 2).wait_recv()
        key_copy(k, 3).start()

    spread(1)
    hand_on(0)

    @pl.loop(2, groups)
    def _(k):
        spread(k)
        hand_on(k - 1)
        score(k - 2)

    hand_on(groups - 1)
    score(groups - 2)
    score(groups - 1)
    tot_mine[ITERS - 1] = 1.0 / tot_mine[ITERS - 1]

    @pl.loop(0, groups)
    def _(k):
        w_all[k] = (raw[k] * tot_mine[ITERS - 1]).astype(jnp.bfloat16)

    for t in range(ITERS):
        mixed[...] = jnp.dot(near[t, 0], w_all[0], preferred_element_type=jnp.float32)

        @pl.loop(1, groups)
        def _(k):
            label_copy(t, k).wait_recv()
            mixed[...] += jnp.dot(near[t, k], w_all[k], preferred_element_type=jnp.float32)

        shifted = mixed[...] + seeds[...] + label_floor
        if t + 1 < ITERS:
            squared = shifted * shifted
            mixed[...] = squared
            tot_mine[t] = jnp.sum(squared, axis=0, keepdims=True)
            for j in range(1, splits):
                total_copy(t, j).start()
            for j in range(1, splits):
                total_copy(t, j).wait_recv()
            total = tot_mine[t]
            for j in range(1, splits):
                total = total + tot_got[t, j]
            soft = (mixed[...] / total).astype(jnp.bfloat16)
            for b in range(blocks):
                fresh[t, b] = soft[:, b * block_rows:(b + 1) * block_rows]

            @pl.loop(1, groups)
            def _(k):
                for s in range(slots):
                    stage_l[t + 1, k, :, s * block_rows:(s + 1) * block_rows] = fresh[t, pick(k, s)]
                label_copy(t + 1, k).start()

            for s in range(slots):
                near[t + 1, 0, :, s * block_rows:(s + 1) * block_rows] = fresh[t, pick(0, s)]
        else:
            for m in range(splits):
                fin_out[m] = shifted[:, m * own:(m + 1) * own]
            for j in range(1, splits):
                final_copy(j).start()
            out[member] = fin_out[member]

    for j in range(1, splits):
        final_copy(j).wait_recv()
        final_copy(j).wait_send()
        query_copy(j).wait_send()
        pre_copy(j).wait_send()
        key_copy(0, j).wait_send()
        for t in range(ITERS - 1):
            total_copy(t, j).wait_send()

    @pl.loop(1, groups)
    def _(k):
        rank_copy(k).wait_send()
        unit_copy(k).wait_send()
        for j in range(1, splits):
            key_copy(k, j).wait_send()
        for t in range(ITERS):
            label_copy(t, k).wait_send()


def fused(groups, splits, slots, ranks, emb, prior, seeds):
    blocks, width, block_rows = emb.shape
    fam = prior.shape[1]
    rows = blocks * block_rows
    pair = slots * block_rows
    own = rows // splits
    vmem = pl.BlockSpec(memory_space=pltpu.VMEM)
    dma = pltpu.SemaphoreType.DMA
    return pl.pallas_call(
        functools.partial(propagate, groups, splits, slots),
        out_shape=jax.ShapeDtypeStruct((splits, fam, own), jnp.float32),
        in_specs=[vmem] * 4,
        out_specs=vmem,
        scratch_shapes=[
            pltpu.VMEM((blocks, width, block_rows), jnp.bfloat16),
            pltpu.VMEM((blocks, fam, block_rows), jnp.bfloat16),
            pltpu.VMEM((2, blocks, block_rows), jnp.float32),
            pltpu.VMEM((splits, 2, blocks, block_rows), jnp.float32),
            pltpu.VMEM((groups, 1, 128), jnp.int32),
            pltpu.SMEM((groups, 1, 128), jnp.int32),
            pltpu.VMEM((splits * width, rows), jnp.bfloat16),
            pltpu.VMEM((groups, splits * width, pair), jnp.bfloat16),
            pltpu.VMEM((pair, splits * width), jnp.bfloat16),
            pltpu.VMEM((groups, pair, rows), jnp.float32),
            pltpu.VMEM((groups, pair, rows), jnp.bfloat16),
            pltpu.VMEM((ITERS, groups, fam, pair), jnp.bfloat16),
            pltpu.VMEM((groups, width, pair), jnp.bfloat16),
            pltpu.VMEM((ITERS, groups, fam, pair), jnp.bfloat16),
            pltpu.VMEM((fam, rows), jnp.float32),
            pltpu.VMEM((ITERS - 1, blocks, fam, block_rows), jnp.bfloat16),
            pltpu.VMEM((ITERS, 1, rows), jnp.float32),
            pltpu.VMEM((ITERS - 1, splits, 1, rows), jnp.float32),
            pltpu.VMEM((splits, fam, own), jnp.float32),
            dma((groups,)), dma((groups,)),
            dma((ITERS, groups)), dma((ITERS, groups)),
            dma((splits,)), dma((splits,)),
            dma((groups, splits)), dma((groups, splits)),
            dma((ITERS - 1, splits)), dma((ITERS - 1, splits)),
            dma((splits,)), dma((splits,)),
            dma((splits,)), dma((splits,)), dma((groups,)), dma((groups,)), dma((1,)),
        ],
        compiler_params=pltpu.CompilerParams(
            collective_id=0, has_side_effects=True, vmem_limit_bytes=40 * 1024 * 1024
        ),
    )(ranks, emb, prior, seeds)


def finish(mine, fam_all):
    total = jnp.sum(mine * mine, axis=-2, keepdims=True)
    return 2.0 * jnp.log(mine) - jnp.log(total) + jnp.log(jnp.float32(fam_all))


def shards(embeddings, prior, neighbours, seed_mask, families):
    groups = lax.axis_size("rows")
    splits = lax.axis_size("dim")
    member = lax.axis_index("dim")
    blocks = neighbours.shape[0]
    links = neighbours.shape[1]
    width = embeddings.shape[1]
    block_rows = embeddings.shape[2]
    fam_part = prior.shape[1]
    fam_all = fam_part * splits
    slots = blocks // 4
    owned = blocks // splits
    candidates = groups * slots
    shared = candidates == links and splits == 4
    places = jnp.arange(blocks, dtype=jnp.int32)
    everything = groups * blocks
    hits = neighbours[:, :, None] == jnp.arange(everything, dtype=jnp.int32)[None, None, :]
    named = jnp.any(hits, axis=(0, 1)).reshape(groups, blocks)
    upto = (places[None, :] <= places[:, None]).astype(jnp.int32)
    order = jnp.sum(named.astype(jnp.int32)[:, None, :] * upto[None, :, :], axis=2) - 1
    chosen = named[:, None, :] & (order[:, None, :] == jnp.arange(slots, dtype=jnp.int32)[None, :, None])
    ranked = jnp.sum(jnp.where(chosen, places[None, None, :], 0), axis=2)
    hot = families.reshape(blocks, 1, block_rows) - member * fam_part
    seeds = jnp.where(
        hot == jnp.arange(fam_part, dtype=jnp.int32)[None, :, None],
        seed_weight * seed_mask.astype(jnp.float32).reshape(blocks, 1, block_rows),
        0.0,
    )
    if shared:
        seeds = jnp.transpose(seeds, (1, 0, 2)).reshape(fam_part, blocks * block_rows)
        ranks = jnp.pad(ranked, ((0, 0), (0, 128 - slots)))[:, None, :]
        mine = fused(groups, splits, slots, ranks, embeddings, prior, seeds)
        return jnp.transpose(finish(mine.reshape(fam_all, owned * block_rows), fam_all))
    wanted = lax.all_to_all(ranked, "rows", split_axis=0, concat_axis=0, tiled=True)
    local_squares = jnp.sum(embeddings * embeddings, axis=1)
    raised_prior = jnp.exp(prior)
    local_total = jnp.sum(raised_prior, axis=1)
    squares, prior_total = lax.psum((local_squares, local_total), "dim")
    unit_blocks = (embeddings * lax.rsqrt(squares + norm_eps)[:, None, :]).astype(jnp.bfloat16)
    labels = (raised_prior / prior_total[:, None, :]).astype(jnp.bfloat16)
    both = jnp.concatenate([unit_blocks, labels], axis=1)
    queries = lax.all_gather(unit_blocks, "dim", axis=1, tiled=True)
    arrived = lax.all_to_all(both[wanted], "rows", split_axis=0, concat_axis=0, tiled=True).reshape(
        candidates, width + fam_part, block_rows
    )
    came = arrived[:, width:]
    keys = lax.all_gather(arrived[:, :width], "dim", axis=1, tiled=True)
    owner = neighbours // blocks
    within = neighbours % blocks
    match = (within[:, :, None] == places[None, None, :]).astype(jnp.int32)
    flat = owner * slots + jnp.sum(match * order[owner], axis=2)

    def block_weights(packed):
        query, listed = packed
        cosine = jnp.einsum(
            "sek,er->skr", keys[listed], query, preferred_element_type=jnp.float32
        )
        raised = jnp.exp(sharpness * (cosine - 1.0))
        return (raised / jnp.sum(raised, axis=(0, 1), keepdims=True)).astype(jnp.bfloat16)

    weights = lax.map(block_weights, (queries, flat))
    shifted = seeds
    for sweep in range(ITERS):
        if sweep > 0:
            came = lax.all_to_all(
                labels[wanted], "rows", split_axis=0, concat_axis=0, tiled=True
            ).reshape(candidates, fam_part, block_rows)
        near = came

        def block_mix(packed):
            weight, listed = packed
            return jnp.einsum(
                "sfk,skr->fr", near[listed], weight, preferred_element_type=jnp.float32
            )

        mixed = lax.map(block_mix, (weights, flat))
        shifted = mixed + seeds + label_floor
        if sweep + 1 < ITERS:
            squared = shifted * shifted
            total = lax.psum(jnp.sum(squared, axis=1), "dim")
            labels = (squared / total[:, None, :]).astype(jnp.bfloat16)
    mine = lax.all_to_all(shifted, "dim", split_axis=0, concat_axis=1, tiled=True)
    result = finish(mine, fam_all)
    return jnp.transpose(result, (0, 2, 1)).reshape(owned * block_rows, fam_all)


def solution(mesh):
    return jax.shard_map(
        shards,
        mesh=mesh,
        in_specs=(
            P("rows", "dim", None),
            P("rows", "dim", None),
            P("rows", None),
            P("rows"),
            P("rows"),
        ),
        out_specs=P(("rows", "dim"), None),
        check_vma=False,
    )
```

```python
import functools

import jax
import jax.numpy as jnp
from jax import lax
from jax.experimental import pallas as pl
from jax.experimental.pallas import tpu as pltpu
from jax.sharding import PartitionSpec as P

ITERS = 3


sharpness = 16.0
seed_weight = 0.5
label_floor = 0.001
norm_eps = 1e-06


def propagate(
    groups, splits, slots,
    ranks, emb, prior, known, kinds, out,
    seeds,
    unit, labels, pre_mine, pre_got, rank_got, wanted,
    q_all, k_all, turned, raw, w_all, near, stage_u, stage_l, mixed, fresh, tot_mine, tot_got, fin_out,
    send_u, recv_u, send_l, recv_l, send_q, recv_q, send_k, recv_k, send_t, recv_t, send_f, recv_f,
    send_p, recv_p, send_r, recv_r, move,
):
    me = lax.axis_index("rows")
    member = lax.axis_index("dim")
    blocks, width, block_rows = emb.shape
    rows = blocks * block_rows
    own = rows // splits
    bar = pltpu.get_barrier_semaphore()

    def row_peer(k):
        return {"rows": lax.rem(me + k, groups)}

    mate = member + 1 - 2 * lax.rem(member, 2)
    others = (member, mate, lax.rem(member + 2, splits), lax.rem(mate + 2, splits))

    def dim_peer(j):
        return {"dim": others[j]}

    def remote(src, dst, send, recv, peer):
        return pltpu.make_async_remote_copy(
            src_ref=src, dst_ref=dst, send_sem=send, recv_sem=recv,
            device_id=peer, device_id_type=pl.DeviceIdType.MESH,
        )

    def unit_copy(k):
        return remote(
            stage_u.at[k], k_all.at[k, pl.ds(0, width), :], send_u.at[k], recv_u.at[k], row_peer(k)
        )

    def label_copy(t, k):
        return remote(
            stage_l.at[t, k], near.at[t, k], send_l.at[t, k], recv_l.at[t, k], row_peer(k)
        )

    def query_copy(j):
        return remote(
            q_all.at[pl.ds((j // 3) * 2 * width, width), :], q_all.at[pl.ds(j * width, width), :],
            send_q.at[j], recv_q.at[j], dim_peer(2 if j == 2 else 1),
        )

    def key_copy(k, j):
        return remote(
            k_all.at[k, pl.ds((j // 3) * 2 * width, width), :],
            k_all.at[k, pl.ds(j * width, width), :],
            send_k.at[k, j], recv_k.at[k, j], dim_peer(2 if j == 2 else 1),
        )

    def total_copy(t, j):
        return remote(
            tot_mine.at[t], tot_got.at[t, j], send_t.at[t, j], recv_t.at[t, j], dim_peer(j)
        )

    def pre_copy(j):
        return remote(pre_mine, pre_got.at[j], send_p.at[j], recv_p.at[j], dim_peer(j))

    def rank_copy(k):
        return remote(
            ranks.at[lax.rem(me + k, groups)], rank_got.at[me], send_r.at[k], recv_r.at[k],
            row_peer(k),
        )

    def final_copy(j):
        return remote(
            fin_out.at[others[j]], out.at[member], send_f.at[j], recv_f.at[j],
            dim_peer(j),
        )

    for k in range(1, groups):
        pl.semaphore_signal(bar, inc=1, device_id=row_peer(k), device_id_type=pl.DeviceIdType.MESH)
    for j in range(1, splits):
        pl.semaphore_signal(bar, inc=1, device_id=dim_peer(j), device_id_type=pl.DeviceIdType.MESH)

    rank_got[me] = ranks[me]
    for b in range(blocks):
        values = emb[b]
        pre_mine[0, b:b + 1, :] = jnp.sum(values * values, axis=0, keepdims=True)
        pre_mine[1, b:b + 1, :] = jnp.sum(jnp.exp(prior[b]), axis=0, keepdims=True)
    pl.semaphore_wait(bar, groups + splits - 2)
    for k in range(1, groups):
        rank_copy(k).start()
    for j in range(1, splits):
        pre_copy(j).start()
    for j in range(1, splits):
        pre_copy(j).wait_recv()
    sums = pre_mine[...]
    for j in range(1, splits):
        sums = sums + pre_got[j]
    scale = lax.rsqrt(sums[0] + norm_eps)
    for b in range(blocks):
        slices = (emb[b] * scale[b:b + 1, :]).astype(jnp.bfloat16)
        unit[b] = slices
        q_all[0:width, b * block_rows:(b + 1) * block_rows] = slices
    for j in (2, 1):
        query_copy(j).start()
    for k in range(1, groups):
        rank_copy(k).wait_recv()
    down = pltpu.make_async_copy(rank_got, wanted, move.at[0])
    down.start()
    down.wait()

    def pick(k, s):
        return wanted[lax.rem(me + k, groups), 0, s]

    @pl.loop(1, groups)
    def _(k):
        for s in range(slots):
            stage_u[k, :, s * block_rows:(s + 1) * block_rows] = unit[pick(k, s)]
        unit_copy(k).start()

    for s in range(slots):
        k_all[0, 0:width, s * block_rows:(s + 1) * block_rows] = unit[pick(0, s)]
    for j in (2, 1):
        key_copy(0, j).start()
    for b in range(blocks):
        labels[b] = (jnp.exp(prior[b]) / sums[1, b:b + 1, :]).astype(jnp.bfloat16)
    for s in range(slots):
        near[0, 0, :, s * block_rows:(s + 1) * block_rows] = labels[pick(0, s)]

    @pl.loop(1, groups)
    def _(k):
        for s in range(slots):
            stage_l[0, k, :, s * block_rows:(s + 1) * block_rows] = labels[pick(k, s)]

    family = lax.broadcasted_iota(jnp.int32, seeds.shape, 0) + member * seeds.shape[0]
    seeds[...] = jnp.where(
        kinds[...] == family, seed_weight * known[...].astype(jnp.float32), 0.0
    )
    query_copy(2).wait_recv()
    query_copy(3).start()
    query_copy(1).wait_recv()
    query_copy(3).wait_recv()
    tot_mine[ITERS - 1] = jnp.zeros((1, rows), jnp.float32)

    def score(k):
        key_copy(k, 1).wait_recv()
        key_copy(k, 3).wait_recv()
        turned[...] = k_all[k].T

        @pl.loop(0, splits)
        def _(c):
            cols = pl.ds(pl.multiple_of(c * own, own), own)
            cosine = lax.dot_general(
                turned[...], q_all[:, cols], (((1,), (0,)), ((), ())),
                preferred_element_type=jnp.float32,
            )
            raised = jnp.exp(sharpness * (cosine - 1.0))
            raw[k, :, cols] = raised
            tot_mine[ITERS - 1, :, cols] += jnp.sum(raised, axis=0, keepdims=True)

    def spread(k):
        unit_copy(k).wait_recv()
        key_copy(k, 2).start()
        key_copy(k, 1).start()
        label_copy(0, k).start()

    def hand_on(k):
        key_copy(k, 2).wait_recv()
        key_copy(k, 3).start()

    spread(1)
    hand_on(0)

    @pl.loop(2, groups)
    def _(k):
        spread(k)
        hand_on(k - 1)
        score(k - 2)

    hand_on(groups - 1)
    score(groups - 2)
    score(groups - 1)
    tot_mine[ITERS - 1] = 1.0 / tot_mine[ITERS - 1]

    @pl.loop(0, groups)
    def _(k):
        w_all[k] = (raw[k] * tot_mine[ITERS - 1]).astype(jnp.bfloat16)

    for t in range(ITERS):
        mixed[...] = jnp.dot(near[t, 0], w_all[0], preferred_element_type=jnp.float32)

        @pl.loop(1, groups)
        def _(k):
            label_copy(t, k).wait_recv()
            mixed[...] += jnp.dot(near[t, k], w_all[k], preferred_element_type=jnp.float32)

        shifted = mixed[...] + seeds[...] + label_floor
        if t + 1 < ITERS:
            squared = shifted * shifted
            mixed[...] = squared
            tot_mine[t] = jnp.sum(squared, axis=0, keepdims=True)
            for j in range(1, splits):
                total_copy(t, j).start()
            for j in range(1, splits):
                total_copy(t, j).wait_recv()
            total = tot_mine[t]
            for j in range(1, splits):
                total = total + tot_got[t, j]
            soft = (mixed[...] / total).astype(jnp.bfloat16)
            for b in range(blocks):
                fresh[t, b] = soft[:, b * block_rows:(b + 1) * block_rows]

            @pl.loop(1, groups)
            def _(k):
                for s in range(slots):
                    stage_l[t + 1, k, :, s * block_rows:(s + 1) * block_rows] = fresh[t, pick(k, s)]
                label_copy(t + 1, k).start()

            for s in range(slots):
                near[t + 1, 0, :, s * block_rows:(s + 1) * block_rows] = fresh[t, pick(0, s)]
        else:
            for m in range(splits):
                fin_out[m] = shifted[:, m * own:(m + 1) * own]
            for j in range(1, splits):
                final_copy(j).start()
            out[member] = fin_out[member]

    for j in range(1, splits):
        final_copy(j).wait_recv()
        final_copy(j).wait_send()
        query_copy(j).wait_send()
        pre_copy(j).wait_send()
        key_copy(0, j).wait_send()
        for t in range(ITERS - 1):
            total_copy(t, j).wait_send()

    @pl.loop(1, groups)
    def _(k):
        rank_copy(k).wait_send()
        unit_copy(k).wait_send()
        for j in range(1, splits):
            key_copy(k, j).wait_send()
        for t in range(ITERS):
            label_copy(t, k).wait_send()


def fused(groups, splits, slots, ranks, emb, prior, known, kinds):
    blocks, width, block_rows = emb.shape
    fam = prior.shape[1]
    rows = blocks * block_rows
    pair = slots * block_rows
    own = rows // splits
    vmem = pl.BlockSpec(memory_space=pltpu.VMEM)
    dma = pltpu.SemaphoreType.DMA
    return pl.pallas_call(
        functools.partial(propagate, groups, splits, slots),
        out_shape=jax.ShapeDtypeStruct((splits, fam, own), jnp.float32),
        in_specs=[vmem] * 5,
        out_specs=vmem,
        scratch_shapes=[
            pltpu.VMEM((fam, rows), jnp.float32),
            pltpu.VMEM((blocks, width, block_rows), jnp.bfloat16),
            pltpu.VMEM((blocks, fam, block_rows), jnp.bfloat16),
            pltpu.VMEM((2, blocks, block_rows), jnp.float32),
            pltpu.VMEM((splits, 2, blocks, block_rows), jnp.float32),
            pltpu.VMEM((groups, 1, 128), jnp.int32),
            pltpu.SMEM((groups, 1, 128), jnp.int32),
            pltpu.VMEM((splits * width, rows), jnp.bfloat16),
            pltpu.VMEM((groups, splits * width, pair), jnp.bfloat16),
            pltpu.VMEM((pair, splits * width), jnp.bfloat16),
            pltpu.VMEM((groups, pair, rows), jnp.float32),
            pltpu.VMEM((groups, pair, rows), jnp.bfloat16),
            pltpu.VMEM((ITERS, groups, fam, pair), jnp.bfloat16),
            pltpu.VMEM((groups, width, pair), jnp.bfloat16),
            pltpu.VMEM((ITERS, groups, fam, pair), jnp.bfloat16),
            pltpu.VMEM((fam, rows), jnp.float32),
            pltpu.VMEM((ITERS - 1, blocks, fam, block_rows), jnp.bfloat16),
            pltpu.VMEM((ITERS, 1, rows), jnp.float32),
            pltpu.VMEM((ITERS - 1, splits, 1, rows), jnp.float32),
            pltpu.VMEM((splits, fam, own), jnp.float32),
            dma((groups,)), dma((groups,)),
            dma((ITERS, groups)), dma((ITERS, groups)),
            dma((splits,)), dma((splits,)),
            dma((groups, splits)), dma((groups, splits)),
            dma((ITERS - 1, splits)), dma((ITERS - 1, splits)),
            dma((splits,)), dma((splits,)),
            dma((splits,)), dma((splits,)), dma((groups,)), dma((groups,)), dma((1,)),
        ],
        compiler_params=pltpu.CompilerParams(
            collective_id=0, has_side_effects=True, vmem_limit_bytes=40 * 1024 * 1024
        ),
    )(ranks, emb, prior, known, kinds)


def finish(mine, fam_all):
    total = jnp.sum(mine * mine, axis=-2, keepdims=True)
    return 2.0 * jnp.log(mine) - jnp.log(total) + jnp.log(jnp.float32(fam_all))


def shards(embeddings, prior, neighbours, seed_mask, families):
    groups = lax.axis_size("rows")
    splits = lax.axis_size("dim")
    member = lax.axis_index("dim")
    blocks = neighbours.shape[0]
    links = neighbours.shape[1]
    width = embeddings.shape[1]
    block_rows = embeddings.shape[2]
    fam_part = prior.shape[1]
    fam_all = fam_part * splits
    slots = blocks // 4
    owned = blocks // splits
    candidates = groups * slots
    shared = candidates == links and splits == 4
    places = jnp.arange(blocks, dtype=jnp.int32)
    everything = groups * blocks
    hits = neighbours[:, :, None] == jnp.arange(everything, dtype=jnp.int32)[None, None, :]
    named = jnp.any(hits, axis=(0, 1)).reshape(groups, blocks)
    upto = (places[None, :] <= places[:, None]).astype(jnp.int32)
    order = jnp.sum(named.astype(jnp.int32)[:, None, :] * upto[None, :, :], axis=2) - 1
    chosen = named[:, None, :] & (order[:, None, :] == jnp.arange(slots, dtype=jnp.int32)[None, :, None])
    ranked = jnp.sum(jnp.where(chosen, places[None, None, :], 0), axis=2)
    if shared:
        ranks = jnp.pad(ranked, ((0, 0), (0, 128 - slots)))[:, None, :]
        mine = fused(groups, splits, slots, ranks, embeddings, prior, seed_mask[None, :], families[None, :])
        return jnp.transpose(finish(mine.reshape(fam_all, owned * block_rows), fam_all))
    hot = families.reshape(blocks, 1, block_rows) - member * fam_part
    seeds = jnp.where(
        hot == jnp.arange(fam_part, dtype=jnp.int32)[None, :, None],
        seed_weight * seed_mask.astype(jnp.float32).reshape(blocks, 1, block_rows),
        0.0,
    )
    wanted = lax.all_to_all(ranked, "rows", split_axis=0, concat_axis=0, tiled=True)
    local_squares = jnp.sum(embeddings * embeddings, axis=1)
    raised_prior = jnp.exp(prior)
    local_total = jnp.sum(raised_prior, axis=1)
    squares, prior_total = lax.psum((local_squares, local_total), "dim")
    unit_blocks = (embeddings * lax.rsqrt(squares + norm_eps)[:, None, :]).astype(jnp.bfloat16)
    labels = (raised_prior / prior_total[:, None, :]).astype(jnp.bfloat16)
    both = jnp.concatenate([unit_blocks, labels], axis=1)
    queries = lax.all_gather(unit_blocks, "dim", axis=1, tiled=True)
    arrived = lax.all_to_all(both[wanted], "rows", split_axis=0, concat_axis=0, tiled=True).reshape(
        candidates, width + fam_part, block_rows
    )
    came = arrived[:, width:]
    keys = lax.all_gather(arrived[:, :width], "dim", axis=1, tiled=True)
    owner = neighbours // blocks
    within = neighbours % blocks
    match = (within[:, :, None] == places[None, None, :]).astype(jnp.int32)
    flat = owner * slots + jnp.sum(match * order[owner], axis=2)

    def block_weights(packed):
        query, listed = packed
        cosine = jnp.einsum(
            "sek,er->skr", keys[listed], query, preferred_element_type=jnp.float32
        )
        raised = jnp.exp(sharpness * (cosine - 1.0))
        return (raised / jnp.sum(raised, axis=(0, 1), keepdims=True)).astype(jnp.bfloat16)

    weights = lax.map(block_weights, (queries, flat))
    shifted = seeds
    for sweep in range(ITERS):
        if sweep > 0:
            came = lax.all_to_all(
                labels[wanted], "rows", split_axis=0, concat_axis=0, tiled=True
            ).reshape(candidates, fam_part, block_rows)
        near = came

        def block_mix(packed):
            weight, listed = packed
            return jnp.einsum(
                "sfk,skr->fr", near[listed], weight, preferred_element_type=jnp.float32
            )

        mixed = lax.map(block_mix, (weights, flat))
        shifted = mixed + seeds + label_floor
        if sweep + 1 < ITERS:
            squared = shifted * shifted
            total = lax.psum(jnp.sum(squared, axis=1), "dim")
            labels = (squared / total[:, None, :]).astype(jnp.bfloat16)
    mine = lax.all_to_all(shifted, "dim", split_axis=0, concat_axis=1, tiled=True)
    result = finish(mine, fam_all)
    return jnp.transpose(result, (0, 2, 1)).reshape(owned * block_rows, fam_all)


def solution(mesh):
    return jax.shard_map(
        shards,
        mesh=mesh,
        in_specs=(
            P("rows", "dim", None),
            P("rows", "dim", None),
            P("rows", None),
            P("rows"),
            P("rows"),
        ),
        out_specs=P(("rows", "dim"), None),
        check_vma=False,
    )
```
